768 devices in a mesh: row: 12 (over z), col: 64 (over y, x, core).
Axes of the slice: x: 4, y: 8, z: 12, core: 2. Of those that a mesh axis runs over, the one named last changes fastest.
Arguments:
- features_t: bfloat16 [128, 393216], P('col', 'row'), may hold values from -6 to 6
- adjacency: int32 [12, 128, 128, 128], P('row'), may hold values from 0 to 3
- tile_dst: int32 [12, 128], P('row'), may hold values from 0 to 255
- tile_peer: int32 [12, 128], P('row'), may hold values from 0 to 11
- tile_slot: int32 [12, 128], P('row'), may hold values from 0 to 7, as said below
- offers: int32 [12, 12, 8], P('row'), may hold values from 0 to 255, as said below
- labels: int32 [393216], P(('row', 'col')), may hold values from 0 to 171
- w_self: bfloat16 [128, 256], replicated, may hold values from -0.5 to 0.5
- w_neigh: bfloat16 [128, 256], replicated, may hold values from -0.5 to 0.5
- w_class: bfloat16 [256, 172], replicated, may hold values from -0.375 to 0.375
Outputs:
- grad_features: bfloat16 [128, 393216], P('col', 'row')
- grad_self: float32 [128, 256], P('col')
- grad_neigh: float32 [128, 256], P('col')
- grad_class: float32 [256, 172], P('col')
The draws below stay inside these ranges and needn't reach their ends.
Inputs may be any that keep to these rules, and one draw needn't show every extreme that they name: `tile_slot`: some tile of every row index reads slot 7. `offers`: the 8 block ids that one row index provides to one requester are distinct.
All inputs are finite; a program needn't handle non-finite values.
Results may differ from the reference program's by a relative error of at most 0.014.
Values may be sent and summed in bfloat16 or wider, within the bound.
A program may use at most 32 MiB of HBM per device.

```python
import jax
import jax.numpy as jnp
from jax import lax

F = 128
H = 256
C = 172
BLK = 128
NBR = 256
NT = 128
SLOTS = 8
NODES = 393216
N_ROW = 12


def shared_graph(key):
    subkeys = jax.random.split(key, 8)
    row_ids = jnp.arange(N_ROW, dtype=jnp.int32)
    counts = jax.random.randint(subkeys[0], (N_ROW, N_ROW), 1, SLOTS + 1)
    forced = row_ids[None, :] == (row_ids[:, None] + 1) % N_ROW
    counts = jnp.where(forced, SLOTS, counts)
    scores = jax.random.randint(subkeys[1], (N_ROW, N_ROW, NBR), 0, 2 ** 20) * NBR + jnp.arange(NBR, dtype=jnp.int32)
    ranking = jnp.argsort(scores, axis=2)
    requests = ranking[:, :, :SLOTS].astype(jnp.int32)
    tile_dst = jax.random.randint(subkeys[2], (N_ROW, NT), 0, NBR)
    tile_peer = jax.random.randint(subkeys[3], (N_ROW, NT), 0, N_ROW)
    live_slots = jnp.take_along_axis(counts, tile_peer, axis=1)
    tile_slot = jax.random.randint(subkeys[4], (N_ROW, NT), 0, live_slots)
    first_tile = jnp.arange(NT, dtype=jnp.int32)[None, :] == 0
    tile_peer = jnp.where(first_tile, ((row_ids + 1) % N_ROW)[:, None], tile_peer)
    tile_slot = jnp.where(first_tile, SLOTS - 1, tile_slot)
    weights = jax.random.randint(subkeys[5], (N_ROW, NT, BLK, BLK), 1, 4)
    present = jax.random.randint(subkeys[6], (N_ROW, NT, BLK, BLK), 0, 8) == 0
    isolated = jax.random.randint(subkeys[7], (N_ROW, NBR, BLK), 0, 16) == 0
    isolated_tiles = jax.vmap(lambda table, picks: jnp.take(table, picks, axis=0))(isolated, tile_dst)
    adjacency = jnp.where(present & jnp.logical_not(isolated_tiles)[:, :, :, None], weights, 0)
    return (requests.astype(jnp.int32), tile_dst.astype(jnp.int32), tile_peer.astype(jnp.int32), tile_slot.astype(jnp.int32), adjacency.astype(jnp.int32))


def draw_adjacency(key, part):
    return shared_graph(key)[4]


def draw_tile_dst(key, part):
    return shared_graph(key)[1]


def draw_tile_peer(key, part):
    return shared_graph(key)[2]


def draw_tile_slot(key, part):
    return shared_graph(key)[3]


def draw_offers(key, part):
    return jnp.transpose(shared_graph(key)[0], (1, 0, 2))


def plant(entries, own_key, low, high):
    place = [jax.random.randint(jax.random.fold_in(own_key, axis), (), 0, length) for axis, length in enumerate(entries.shape)]
    widest = entries.shape.index(max(entries.shape))
    beside = place[:widest] + [(place[widest] + 1) % entries.shape[widest]] + place[widest + 1:]
    return entries.at[tuple(place)].set(low).at[tuple(beside)].set(high)


def levels(own_key, shape, cuts, least, largest):
    def one(position, blocks):
        steps = jax.random.uniform(jax.random.fold_in(jax.random.fold_in(own_key, 6), position), (blocks,), jnp.float32, least / len(cuts), largest / len(cuts))
        return jnp.repeat(jnp.exp(steps), shape[position] // blocks).reshape((-1,) + (1,) * (len(shape) - position - 1))

    gain = one(*cuts[0])
    for cut in cuts[1:]:
        gain = gain * one(*cut)
    return gain


def normal_values(own_key, dims, spread, bound, cuts=(), kind=jnp.bfloat16):
    result = spread * jax.random.normal(own_key, dims, jnp.float32)
    if cuts:
        result = result * levels(own_key, dims, cuts, -0.22, 0.18)
    return jnp.clip(result, -bound, bound).astype(kind)


def setup_inputs(seed: int = 0) -> dict:
    key_list = jax.random.split(jax.random.key(seed), 11)
    return {
        "features_t": normal_values(key_list[0], (F, NODES), 1.0, 6.0, ((0, 64), (1, 12))),
        "adjacency": draw_adjacency(jax.random.fold_in(key_list[10], 71), 0),
        "tile_dst": draw_tile_dst(jax.random.fold_in(key_list[10], 71), 0),
        "tile_peer": draw_tile_peer(jax.random.fold_in(key_list[10], 71), 0),
        "tile_slot": draw_tile_slot(jax.random.fold_in(key_list[10], 71), 0),
        "offers": draw_offers(jax.random.fold_in(key_list[10], 71), 0),
        "labels": plant(jax.random.randint(key_list[6], (NODES,), 0, C), jax.random.fold_in(key_list[6], 1), 0, C - 1).astype(jnp.int32),
        "w_self": normal_values(key_list[7], (F, H), F ** -0.5, 0.5),
        "w_neigh": normal_values(key_list[8], (F, H), F ** -0.5, 0.5),
        "w_class": normal_values(key_list[9], (H, C), H ** -0.5, 0.375),
    }


def reference(features_t, adjacency, tile_dst, tile_peer, tile_slot, offers, labels, w_self, w_neigh, w_class):
    highest = lax.Precision.HIGHEST
    group_ids = jnp.arange(N_ROW, dtype=jnp.int32)
    block_ids = offers[tile_peer, group_ids[:, None], tile_slot]
    global_source = (tile_peer * NBR + block_ids).astype(jnp.int32)
    feature_blocks = features_t.reshape(F, N_ROW * NBR, BLK).astype(jnp.float32)

    def forward_group(inputs):
        tile_values, dest_block, source_block = inputs
        weights = tile_values.astype(jnp.float32)
        sources = jnp.take(feature_blocks, source_block, axis=1)
        products = jnp.einsum("ftj,tij->fti", sources, weights, precision=highest)
        summed = jnp.zeros((F, NBR, BLK), jnp.float32).at[:, dest_block].add(products)
        degree = jnp.zeros((NBR, BLK), jnp.float32).at[dest_block].add(jnp.sum(weights, axis=2))
        return summed, degree

    summed, degree = lax.map(forward_group, (adjacency, tile_dst, global_source))
    divisor = jnp.maximum(degree.reshape(NODES), 1.0)
    summed_t = jnp.transpose(summed, (1, 0, 2, 3)).reshape(F, NODES)
    agg_t = (summed_t / divisor[None, :]).astype(jnp.bfloat16)
    pre_act = jnp.dot(features_t.T, w_self, preferred_element_type=jnp.float32) + jnp.dot(agg_t.T, w_neigh, preferred_element_type=jnp.float32)
    sigmoid_act = jax.nn.sigmoid(pre_act)
    hidden = (pre_act * sigmoid_act).astype(jnp.bfloat16)
    logits = jnp.dot(hidden, w_class, preferred_element_type=jnp.float32)
    exponent = jnp.exp(logits)
    softmax_rows = exponent / jnp.sum(exponent, axis=1, keepdims=True)
    target = (labels[:, None] == jnp.arange(C, dtype=jnp.int32)[None, :]).astype(jnp.float32)
    dlogits = (softmax_rows - target).astype(jnp.bfloat16)
    back_hidden = jnp.dot(dlogits, w_class.T, preferred_element_type=jnp.float32)
    slope = sigmoid_act * (1.0 + pre_act * (1.0 - sigmoid_act))
    dpre = (back_hidden * slope).astype(jnp.bfloat16)
    factor = NODES ** -0.5
    grad_self = jnp.dot(features_t, dpre, preferred_element_type=jnp.float32) * factor
    grad_neigh = jnp.dot(agg_t, dpre, preferred_element_type=jnp.float32) * factor
    grad_class = jnp.dot(hidden.T, dlogits, preferred_element_type=jnp.float32) * factor
    self_back = jnp.dot(w_self, dpre.T, preferred_element_type=jnp.float32).astype(jnp.bfloat16)
    neigh_back = (jnp.dot(w_neigh, dpre.T, preferred_element_type=jnp.float32) / divisor[None, :]).astype(jnp.bfloat16)
    neigh_groups = jnp.transpose(neigh_back.reshape(F, N_ROW, NBR, BLK), (1, 0, 2, 3))

    def backward_group(running, inputs):
        tile_values, dest_block, source_block, gradient_group = inputs
        dest_rows = jnp.take(gradient_group.astype(jnp.float32), dest_block, axis=1)
        pushed = jnp.einsum("fti,tij->ftj", dest_rows, tile_values.astype(jnp.float32), precision=highest)
        return running.at[:, source_block].add(pushed), None

    landed = lax.scan(backward_group, jnp.zeros((F, N_ROW * NBR, BLK), jnp.float32), (adjacency, tile_dst, global_source, neigh_groups))[0]
    grad_features = (self_back.astype(jnp.float32) + landed.reshape(F, NODES)).astype(jnp.bfloat16)
    return grad_features, grad_self, grad_neigh, grad_class
```

```python
import jax
import jax.numpy as jnp
from jax import lax
from jax.experimental import pallas as pl
from jax.experimental.pallas import tpu as pltpu
from jax.sharding import PartitionSpec as P

MESH = pl.DeviceIdType.MESH


def reduce_kernel(w_ref, out_ref, half, mine, got, rows, send, recv):
    row_count = lax.axis_size("row")
    chip_count = lax.axis_size("col") // 2
    row, col = lax.axis_index("row"), lax.axis_index("col")
    chip, core = col // 2, col % 2
    sibling = (row, chip * 2 + 1 - core)

    def chip_at(step):
        other = lax.rem(chip + step, chip_count)
        return other, (row, other * 2 + core)

    def row_at(step):
        return (lax.rem(row + step, row_count), col)

    barrier = pltpu.get_barrier_semaphore()

    def greet(device):
        pl.semaphore_signal(barrier, inc=1, device_id=device, device_id_type=MESH)

    greet(sibling)

    @pl.loop(1, chip_count)
    def _(step):
        greet(chip_at(step)[1])

    @pl.loop(1, row_count)
    def _(step):
        greet(row_at(step))

    pl.semaphore_wait(barrier, chip_count + row_count - 1)
    swap = pltpu.make_async_remote_copy(
        w_ref.at[1 - core], half, send.at[0], recv.at[0], device_id=sibling, device_id_type=MESH
    )
    swap.start()
    swap.wait()
    mine[...] = w_ref[core] + half[...]
    got[chip] = mine[chip]

    @pl.loop(1, chip_count)
    def _(step):
        other, device = chip_at(step)
        pltpu.make_async_remote_copy(
            mine.at[other], got.at[chip], send.at[1], recv.at[1], device_id=device, device_id_type=MESH
        ).start()

    others = got.at[pl.ds(0, chip_count - 1)]
    pltpu.make_async_copy(others, others, recv.at[1]).wait()
    rows[row] = jnp.sum(got[...], axis=0)

    @pl.loop(1, row_count)
    def _(step):
        pltpu.make_async_remote_copy(
            rows.at[row], rows.at[row], send.at[2], recv.at[2], device_id=row_at(step), device_id_type=MESH
        ).start()

    others_row = rows.at[pl.ds(0, row_count - 1)]
    pltpu.make_async_copy(others_row, others_row, recv.at[2]).wait()
    out_ref[...] = jnp.sum(rows[...], axis=0)
    pltpu.make_async_copy(others, others, send.at[1]).wait()
    pltpu.make_async_copy(others_row, others_row, send.at[2]).wait()


def reduce_weights(weights):
    cores, chips, height, width = weights.shape
    row_count = lax.axis_size("row")
    return pl.pallas_call(
        reduce_kernel,
        out_shape=jax.ShapeDtypeStruct((height, width), jnp.float32),
        in_specs=[pl.BlockSpec(memory_space=pltpu.VMEM)],
        out_specs=pl.BlockSpec(memory_space=pltpu.VMEM),
        scratch_shapes=[
            pltpu.VMEM((chips, height, width), jnp.float32),
            pltpu.VMEM((chips, height, width), jnp.float32),
            pltpu.VMEM((chips, height, width), jnp.float32),
            pltpu.VMEM((row_count, height, width), jnp.float32),
            pltpu.SemaphoreType.DMA((3,)),
            pltpu.SemaphoreType.DMA((3,)),
        ],
        compiler_params=pltpu.CompilerParams(
            collective_id=0, has_side_effects=True, vmem_limit_bytes=16 << 20
        ),
    )(weights)


def body(
    features_t, adjacency, tile_dst, tile_peer, tile_slot, offers, labels, w_self, w_neigh, w_class
):
    highest = lax.Precision.HIGHEST
    row_count = lax.axis_size("row")
    col_count = lax.axis_size("col")
    feat_cols, node_rows = features_t.shape
    block_size = adjacency.shape[2]
    block_count = node_rows // block_size
    slot_count = offers.shape[2]
    rows_here = labels.shape[0]
    class_count = w_class.shape[1]
    tile_weights = adjacency[0].astype(jnp.bfloat16)
    dest_block = tile_dst[0]
    source_slot = tile_peer[0] * slot_count + tile_slot[0]
    dest_onehot = (dest_block[:, None] == jnp.arange(block_count, dtype=jnp.int32)[None, :]).astype(
        jnp.float32
    )
    row_sums = jnp.sum(adjacency[0], axis=2).astype(jnp.float32)
    degree = jnp.dot(dest_onehot.T, row_sums, precision=highest)
    divisor = jnp.maximum(degree, 1.0)
    feature_blocks = features_t.reshape(feat_cols, block_count, block_size)
    outgoing = jnp.take(feature_blocks, offers[0], axis=1)
    incoming = lax.all_to_all(outgoing, "row", split_axis=1, concat_axis=1, tiled=True)
    sources = jnp.take(
        incoming.reshape(feat_cols, row_count * slot_count, block_size), source_slot, axis=1
    )
    products = jnp.einsum("ftj,tij->fti", sources, tile_weights, preferred_element_type=jnp.float32)
    summed = jnp.einsum("fti,tb->fbi", products, dest_onehot, precision=highest)
    aggregate = (summed / divisor[None]).astype(jnp.bfloat16).reshape(feat_cols, node_rows)
    rows_feat, rows_agg = (
        lax.all_to_all(features_t, "col", split_axis=1, concat_axis=0, tiled=True),
        lax.all_to_all(aggregate, "col", split_axis=1, concat_axis=0, tiled=True),
    )
    contract_first = (((0,), (0,)), ((), ()))
    contract_last = (((1,), (1,)), ((), ()))
    contract_inner = (((1,), (0,)), ((), ()))
    pre_act = lax.dot_general(
        rows_feat, w_self, contract_first, preferred_element_type=jnp.float32
    ) + lax.dot_general(rows_agg, w_neigh, contract_first, preferred_element_type=jnp.float32)
    sigmoid_act = jax.nn.sigmoid(pre_act)
    hidden = (pre_act * sigmoid_act).astype(jnp.bfloat16)
    logits = jnp.dot(hidden, w_class, preferred_element_type=jnp.float32)
    exponent = jnp.exp(logits)
    softmax_rows = exponent / jnp.sum(exponent, axis=1, keepdims=True)
    target = (labels[:, None] == jnp.arange(class_count, dtype=jnp.int32)[None, :]).astype(
        jnp.float32
    )
    dlogits = (softmax_rows - target).astype(jnp.bfloat16)
    back_hidden = lax.dot_general(
        dlogits, w_class, contract_last, preferred_element_type=jnp.float32
    )
    slope = sigmoid_act * (1.0 + pre_act * (1.0 - sigmoid_act))
    dpre = (back_hidden * slope).astype(jnp.bfloat16)
    node_total = rows_here * row_count * col_count
    factor = node_total ** (-0.5)
    self_part = (
        lax.dot_general(rows_feat, dpre, contract_inner, preferred_element_type=jnp.float32)
        * factor
    )
    neigh_part = (
        lax.dot_general(rows_agg, dpre, contract_inner, preferred_element_type=jnp.float32) * factor
    )
    class_part = (
        lax.dot_general(hidden, dlogits, contract_first, preferred_element_type=jnp.float32)
        * factor
    )
    self_back = lax.dot_general(
        w_self, dpre, contract_last, preferred_element_type=jnp.float32
    ).astype(jnp.bfloat16)
    my_divisor = lax.dynamic_slice_in_dim(
        divisor.reshape(node_rows), lax.axis_index("col") * rows_here, rows_here, 0
    )
    neigh_back = (
        lax.dot_general(w_neigh, dpre, contract_last, preferred_element_type=jnp.float32)
        / my_divisor[None, :]
    ).astype(jnp.bfloat16)
    cols_self, cols_neigh = (
        lax.all_to_all(self_back, "col", split_axis=0, concat_axis=1, tiled=True),
        lax.all_to_all(neigh_back, "col", split_axis=0, concat_axis=1, tiled=True),
    )
    dest_rows = jnp.take(cols_neigh.reshape(feat_cols, block_count, block_size), dest_block, axis=1)
    pushed = jnp.einsum("fti,tij->ftj", dest_rows, tile_weights, preferred_element_type=jnp.float32)
    slot_onehot = (
        source_slot[:, None] == jnp.arange(row_count * slot_count, dtype=jnp.int32)[None, :]
    ).astype(jnp.float32)
    per_slot = jnp.einsum("ftj,ts->fsj", pushed, slot_onehot, precision=highest).reshape(
        feat_cols, row_count, slot_count, block_size
    )
    returned = lax.all_to_all(per_slot, "row", split_axis=1, concat_axis=1, tiled=True)
    offer_onehot = (
        offers[0].reshape(row_count * slot_count)[:, None]
        == jnp.arange(block_count, dtype=jnp.int32)[None, :]
    ).astype(jnp.float32)
    landed = jnp.einsum(
        "fsj,sb->fbj",
        returned.reshape(feat_cols, row_count * slot_count, block_size),
        offer_onehot,
        precision=highest,
    ).reshape(feat_cols, node_rows)
    grad_features = (cols_self.astype(jnp.float32) + landed).astype(jnp.bfloat16)
    hidden_cols = w_class.shape[0] // col_count
    hidden_units = w_self.shape[1]
    packed = jnp.concatenate(
        [
            self_part.reshape(col_count, feat_cols, hidden_units),
            neigh_part.reshape(col_count, feat_cols, hidden_units),
            jnp.pad(
                class_part.reshape(col_count, hidden_cols, class_count),
                ((0, 0), (0, 0), (0, hidden_units - class_count)),
            ),
        ],
        axis=1,
    )
    total = reduce_weights(
        packed.reshape(col_count // 2, 2, -1, hidden_units).transpose(1, 0, 2, 3)
    )
    grad_self = total[:feat_cols]
    grad_neigh = total[feat_cols : 2 * feat_cols]
    grad_class = total[2 * feat_cols :, :class_count]
    return (grad_features, grad_self, grad_neigh, grad_class)


def solution(mesh):
    in_specs = (
        P("col", "row"),
        P("row", None, None, None),
        P("row", None),
        P("row", None),
        P("row", None),
        P("row", None, None),
        P(("row", "col")),
        P(),
        P(),
        P(),
    )
    out_specs = (P("col", "row"), P("col", None), P("col", None), P("col", None))
    return jax.shard_map(body, mesh=mesh, in_specs=in_specs, out_specs=out_specs, check_vma=False)
```

```python
import functools

import jax
import jax.numpy as jnp
from jax import lax
from jax.experimental import pallas as pl
from jax.experimental.pallas import tpu as pltpu
from jax.sharding import PartitionSpec as P

MESH = pl.DeviceIdType.MESH
F32 = jnp.float32
BF16 = jnp.bfloat16
LANES = 128
CHUNKS = 8

OFFERED, FEATURES, AGGREGATE, NEIGH_BACK, SELF_BACK, RETURNED, SWAP, CHIPS, ROWS, PAIR = range(10)

INNER = (((1,), (0,)), ((), ()))
LAST = (((1,), (1,)), ((), ()))


def dot(a, b, dims=INNER):
    return lax.dot_general(a, b, dims, preferred_element_type=F32)


def split_dot(onehot, values):
    high = values.astype(BF16)
    low = (values - high.astype(F32)).astype(BF16)
    return dot(onehot, high) + dot(onehot, low)


def onehot(condition):
    return jnp.where(condition, 1.0, 0.0).astype(BF16)


def iota(shape, axis):
    return lax.broadcasted_iota(jnp.int32, shape, axis)


def layer_kernel(
    scale,
    feat_ref, adjacency_ref, dst_ref, peer_ref, slot_ref, offers_ref, labels_ref,
    w_self_ref, w_neigh_ref, w_class_ref,
    grad_ref, grad_self_ref, grad_neigh_ref, grad_class_ref,
    raw, tiles,
    offer_pad, pick_offer, put_offer, pick_source, put_source, pick_dest, put_dest, put_degree,
    to_nodes, to_columns,
    w_self_t, w_neigh_t, w_class_p, w_class_t,
    offered, incoming, feat_recv, agg_send, agg_recv, neigh_send, neigh_recv, self_send, self_recv,
    slot_send, slot_recv, weights, half, mine, got, sums, pair,
    gathered, products, degree, x_self, x_neigh,
    tile_sem, send, recv,
):
    row_count, col_count = lax.axis_size("row"), lax.axis_size("col")
    chip_count = col_count // 2
    row, col = lax.axis_index("row"), lax.axis_index("col")
    chip, core = col // 2, col % 2
    sibling = (row, chip * 2 + 1 - core)
    node_rows = col_count * 8
    tile_count = raw.shape[0]
    octs = tile_count // 8
    slot_rows = row_count * 16
    padded = incoming.shape[0] * 16

    def col_at(step):
        other = lax.rem(col + step, col_count)
        return other, (row, other)

    def row_at(step):
        other = lax.rem(row + step, row_count)
        return other, (other, col)

    def chip_at(step):
        other = lax.rem(chip + step, chip_count)
        return other, (row, other * 2 + core)

    def remote(source, target, phase, device):
        return pltpu.make_async_remote_copy(
            source, target, send.at[phase], recv.at[phase], device_id=device, device_id_type=MESH
        )

    def scatter(source, target, phase, count, at, here):
        @pl.loop(1, count)
        def _(step):
            other, device = at(step)
            remote(source.at[other], target.at[here], phase, device).start()

        target[here] = source[here]

    def wait_for(target, count, semaphore):
        others = target.at[pl.ds(0, count - 1)]
        pltpu.make_async_copy(others, others, semaphore).wait()

    barrier = pltpu.get_barrier_semaphore()

    @pl.loop(1, row_count)
    def _(step):
        pl.semaphore_signal(barrier, inc=1, device_id=row_at(step)[1], device_id_type=MESH)

    @pl.loop(1, col_count)
    def _(step):
        pl.semaphore_signal(barrier, inc=1, device_id=col_at(step)[1], device_id_type=MESH)

    per_chunk = tile_count // CHUNKS

    def chunk_copy(part):
        place = pl.ds(part * per_chunk, per_chunk)
        return pltpu.make_async_copy(adjacency_ref.at[0, place], raw.at[place], tile_sem.at[part])

    for part in range(CHUNKS):
        chunk_copy(part).start()

    offer_pad[...] = jnp.zeros_like(offer_pad)
    offer_pad[0:row_count, 0 : offers_ref.shape[2]] = offers_ref[0].astype(F32)
    offer_rows = dot(
        onehot(iota((padded, offer_pad.shape[0]), 0) // 16 == iota((padded, offer_pad.shape[0]), 1)),
        offer_pad[...].astype(BF16),
    )
    place = iota((padded, LANES), 0)
    offer_col = jnp.sum(
        jnp.where(place % 8 == iota((padded, LANES), 1), offer_rows, 0.0), axis=1, keepdims=True
    ).astype(jnp.int32)
    place_col = iota((padded, 1), 0)
    offer_col = (offer_col // 4) * 8 + offer_col % 4 + ((place_col // 8) % 2) * 4
    offer_col = jnp.where(place_col < slot_rows, offer_col, -1)
    pick = jnp.where(offer_col == iota((padded, node_rows), 1), 1.0, 0.0)
    pick_offer[...] = pick.astype(BF16)
    offered[...] = (
        dot(pick_offer[...], feat_ref[...].reshape(node_rows, LANES))
        .astype(BF16)
        .reshape(offered.shape)
    )
    incoming[row_count:] = jnp.zeros_like(incoming[row_count:])
    slot_recv[row_count:] = jnp.zeros_like(slot_recv[row_count:])

    pl.semaphore_wait(barrier, row_count + col_count - 2)
    scatter(offered, incoming, OFFERED, row_count, row_at, row)
    scatter(feat_ref, feat_recv, FEATURES, col_count, col_at, col)

    put_offer[...] = pick.T.astype(BF16)
    dst = dst_ref[...]
    source = peer_ref[...] * 16 + slot_ref[...]
    dst_row = (dst // 4) * 8 + dst % 4
    dst_rows = jnp.concatenate([dst_row, dst_row + 4], axis=1)
    source_rows = jnp.concatenate([source, source + 8], axis=1)
    pairs = dst_rows.shape[1]
    square = iota((pairs, pairs), 0) == iota((pairs, pairs), 1)

    def column(values):
        return jnp.sum(jnp.where(square, values, 0), axis=1, keepdims=True)

    put_dest[...] = onehot(iota((node_rows, pairs), 0) == dst_rows)
    pick_dest[...] = onehot(iota((pairs, node_rows), 1) == column(dst_rows))
    put_source[...] = onehot(iota((padded, pairs), 0) == source_rows)
    pick_source[...] = onehot(iota((pairs, padded), 1) == column(source_rows))
    block_of = iota((node_rows, tile_count), 0)
    put_degree[...] = onehot((block_of // 8) * 4 + block_of % 4 == dst)
    feat_count = col_count * 2
    one, two = iota((node_rows, node_rows), 0), iota((node_rows, node_rows), 1)
    to_nodes[...] = onehot(two == (one % feat_count) * 4 + one // feat_count)
    to_columns[...] = onehot(one == (two % feat_count) * 4 + two // feat_count)
    w_self_t[...] = w_self_ref[...].astype(F32).T.astype(BF16)
    w_neigh_t[...] = w_neigh_ref[...].astype(F32).T.astype(BF16)
    hidden_units, class_count = w_class_ref.shape
    class_rows = w_class_t.shape[0]
    w_class_p[...] = jnp.zeros_like(w_class_p)
    w_class_p[:, 0:class_count] = w_class_ref[...]
    w_class_t[...] = w_class_p[...].astype(F32).T.astype(BF16)[:class_rows]

    for part in range(CHUNKS):
        chunk_copy(part).wait()
        for oct_ in range(part * octs // CHUNKS, (part + 1) * octs // CHUNKS):
            for k in range(8):
                tiles[oct_, k // 2 * LANES : (k // 2 + 1) * LANES, k % 2 * LANES : (k % 2 + 1) * LANES] = (
                    raw[oct_ * 8 + k].astype(F32).astype(BF16)
                )

    wait_for(incoming, row_count, recv.at[OFFERED])
    gathered[...] = dot(pick_source[...], incoming[...].reshape(padded, LANES))
    kinds = iota((24, LANES), 0) % 8
    ones = jnp.ones((8, LANES), F32)
    for oct_ in range(octs):
        lines = jnp.concatenate(
            [gathered[8 * oct_ : 8 * oct_ + 8], gathered[tile_count + 8 * oct_ : tile_count + 8 * oct_ + 8], ones],
            axis=0,
        )
        left = jnp.concatenate(
            [jnp.where(kinds % 2 == half_, lines, 0.0) for half_ in range(2)], axis=1
        ).astype(BF16)
        out = dot(left, tiles[oct_], LAST)
        kept = out[:, 0:LANES]
        for quarter in range(1, 4):
            kept = jnp.where(
                kinds // 2 == quarter, out[:, quarter * LANES : (quarter + 1) * LANES], kept
            )
        for kind in range(3):
            at = kind * tile_count + 8 * oct_
            products[at : at + 8] = kept[8 * kind : 8 * kind + 8]
    divisor = jnp.maximum(split_dot(put_degree[...], products[pairs : pairs + tile_count]), 1.0)
    degree[...] = divisor
    agg_send[...] = (
        (split_dot(put_dest[...], products[0:pairs]) / divisor).astype(BF16).reshape(agg_send.shape)
    )
    scatter(agg_send, agg_recv, AGGREGATE, col_count, col_at, col)

    def node_columns(received, x_ref):
        moved = dot(to_nodes[...], received[...].reshape(node_rows, LANES)).astype(BF16)
        for block in range(4):
            x_ref[:, block * LANES : (block + 1) * LANES] = moved[
                block * feat_count : (block + 1) * feat_count
            ]

    wait_for(feat_recv, col_count, recv.at[FEATURES])
    node_columns(feat_recv, x_self)
    pre_self = dot(w_self_t[...], x_self[...])
    wait_for(agg_recv, col_count, recv.at[AGGREGATE])
    node_columns(agg_recv, x_neigh)

    pre = pre_self + dot(w_neigh_t[...], x_neigh[...])
    sigmoid = 1.0 / (1.0 + jnp.exp(-pre))
    hidden = (pre * sigmoid).astype(BF16)
    logits = dot(w_class_t[...], hidden)
    classes = iota(logits.shape, 0)
    exponent = jnp.where(classes < class_count, jnp.exp(logits), 0.0)
    soft = exponent / jnp.sum(exponent, axis=0, keepdims=True)
    label_row = jnp.concatenate([labels_ref[block : block + 1] for block in range(4)], axis=1)
    dlogits = (soft - jnp.where(classes == label_row, 1.0, 0.0)).astype(BF16)
    slope = sigmoid * (1.0 + pre * (1.0 - sigmoid))
    dpre = (dot(w_class_p[:, 0:class_rows], dlogits) * slope).astype(BF16)

    def block_rows(values):
        stacked = jnp.concatenate(
            [values[:, block * LANES : (block + 1) * LANES] for block in range(4)], axis=0
        )
        return dot(to_columns[...], stacked).astype(BF16).reshape(neigh_send.shape)

    my_degree = degree[pl.ds(pl.multiple_of(col * 8, 8), 8)]
    my_divisor = jnp.concatenate([my_degree[block : block + 1] for block in range(4)], axis=1)
    neigh_send[...] = block_rows((dot(w_neigh_ref[...], dpre) / my_divisor).astype(BF16))
    scatter(neigh_send, neigh_recv, NEIGH_BACK, col_count, col_at, col)
    self_send[...] = block_rows(dot(w_self_ref[...], dpre).astype(BF16))
    scatter(self_send, self_recv, SELF_BACK, col_count, col_at, col)

    both = jnp.concatenate([x_self[...], x_neigh[...]], axis=0)
    one, two = iota((2 * feat_count, 2 * feat_count), 0), iota((2 * feat_count, 2 * feat_count), 1)
    mixed = dot(
        onehot(two == (one // 8) * 4 + one % 4 + ((one // 4) % 2) * feat_count), both
    ).astype(BF16)
    weights[0] = (dot(mixed, dpre, LAST) * scale).reshape(half.shape)
    class_grad = dot(hidden, jnp.concatenate([dlogits, jnp.zeros((hidden_units - class_rows, dlogits.shape[1]), BF16)], axis=0), LAST)
    weights[1] = (class_grad * scale).reshape(half.shape)
    swap = remote(weights.at[1 - core], half, SWAP, sibling)
    swap.start()
    swap.wait()
    mine[...] = weights[core] + half[...]
    scatter(mine, got, CHIPS, chip_count, chip_at, chip)

    wait_for(neigh_recv, col_count, recv.at[NEIGH_BACK])
    gathered[...] = dot(pick_dest[...], neigh_recv[...].reshape(node_rows, LANES))
    kinds = iota((16, LANES), 0) % 8
    for oct_ in range(octs):
        lines = jnp.concatenate(
            [gathered[8 * oct_ : 8 * oct_ + 8], gathered[tile_count + 8 * oct_ : tile_count + 8 * oct_ + 8]],
            axis=0,
        )
        left = jnp.concatenate(
            [jnp.where(kinds // 2 == quarter, lines, 0.0) for quarter in range(4)], axis=1
        ).astype(BF16)
        out = dot(left, tiles[oct_])
        kept = jnp.where(kinds % 2 == 0, out[:, 0:LANES], out[:, LANES : 2 * LANES])
        for kind in range(2):
            at = kind * tile_count + 8 * oct_
            products[at : at + 8] = kept[8 * kind : 8 * kind + 8]
    slot_send[...] = split_dot(put_source[...], products[0:pairs]).reshape(slot_send.shape)
    scatter(slot_send, slot_recv, RETURNED, row_count, row_at, row)

    wait_for(got, chip_count, recv.at[CHIPS])
    sums[row] = jnp.sum(got[...], axis=0)

    @pl.loop(1, row_count)
    def _(step):
        remote(sums.at[row], sums.at[row], ROWS, row_at(step)[1]).start()

    wait_for(self_recv, col_count, recv.at[SELF_BACK])
    wait_for(slot_recv, row_count, recv.at[RETURNED])
    landed = split_dot(put_offer[...], slot_recv[...].reshape(padded, LANES))
    grad_ref[...] = (
        (self_recv[...].reshape(node_rows, LANES).astype(F32) + landed)
        .astype(BF16)
        .reshape(grad_ref.shape)
    )
    wait_for(sums, row_count, recv.at[ROWS])
    pair[core] = jnp.sum(sums[...], axis=0)
    last = remote(pair.at[core], pair.at[core], PAIR, sibling)
    last.start()
    last.wait()
    matrices, classes_part = pair[0], pair[1]
    first = core == 0
    grad_self_ref[...] = jnp.where(first, matrices[0:2], matrices[2:4])
    grad_neigh_ref[...] = jnp.where(first, matrices[4:6], matrices[6:8])
    grad_class_ref[...] = jnp.where(first, classes_part[0:4], classes_part[4:8])[:, 0:class_count]

    wait_for(incoming, row_count, send.at[OFFERED])
    for phase in (FEATURES, AGGREGATE, NEIGH_BACK, SELF_BACK):
        wait_for(feat_recv, col_count, send.at[phase])
    wait_for(slot_recv, row_count, send.at[RETURNED])
    wait_for(got, chip_count, send.at[CHIPS])
    wait_for(sums, row_count, send.at[ROWS])


def body(
    features_t, adjacency, tile_dst, tile_peer, tile_slot, offers, labels, w_self, w_neigh, w_class
):
    row_count = lax.axis_size("row")
    col_count = lax.axis_size("col")
    feat_cols, node_rows = features_t.shape
    tile_count = adjacency.shape[1]
    hidden_units, class_count = w_class.shape
    feats = feat_cols * col_count
    class_rows = -(-class_count // 16) * 16
    padded = -(-row_count // 8) * 8
    blocks = col_count * 8
    chips = col_count // 2
    rows_here = labels.shape[0]
    scale = (rows_here * row_count * col_count) ** (-0.5)
    by_col = (
        features_t.reshape(feat_cols, col_count, 4, LANES)
        .transpose(1, 0, 2, 3)
        .reshape(col_count, 8, LANES)
    )
    vmem = pl.BlockSpec(memory_space=pltpu.VMEM)
    message = pltpu.VMEM((col_count, 8, LANES), BF16)
    part = pltpu.VMEM((chips, 8, hidden_units), F32)
    grad, grad_self, grad_neigh, grad_class = pl.pallas_call(
        functools.partial(layer_kernel, scale),
        out_shape=(
            jax.ShapeDtypeStruct((col_count, 8, LANES), BF16),
            jax.ShapeDtypeStruct((feat_cols, hidden_units), F32),
            jax.ShapeDtypeStruct((feat_cols, hidden_units), F32),
            jax.ShapeDtypeStruct((hidden_units // col_count, class_count), F32),
        ),
        in_specs=[vmem, pl.BlockSpec(memory_space=pl.ANY)] + [vmem] * 8,
        out_specs=(vmem,) * 4,
        scratch_shapes=[
            pltpu.VMEM((tile_count, LANES, LANES), jnp.int32),
            pltpu.VMEM((tile_count // 8, 4 * LANES, 2 * LANES), BF16),
            pltpu.VMEM((padded, LANES), F32),
            pltpu.VMEM((padded * 16, blocks), BF16),
            pltpu.VMEM((blocks, padded * 16), BF16),
            pltpu.VMEM((2 * tile_count, padded * 16), BF16),
            pltpu.VMEM((padded * 16, 2 * tile_count), BF16),
            pltpu.VMEM((2 * tile_count, blocks), BF16),
            pltpu.VMEM((blocks, 2 * tile_count), BF16),
            pltpu.VMEM((blocks, tile_count), BF16),
            pltpu.VMEM((blocks, blocks), BF16),
            pltpu.VMEM((blocks, blocks), BF16),
            pltpu.VMEM((hidden_units, feats), BF16),
            pltpu.VMEM((hidden_units, feats), BF16),
            pltpu.VMEM((hidden_units, hidden_units), BF16),
            pltpu.VMEM((class_rows, hidden_units), BF16),
            pltpu.VMEM((padded, 16, LANES), BF16),
            pltpu.VMEM((padded, 16, LANES), BF16),
            message, message, message, message, message, message, message,
            pltpu.VMEM((padded, 16, LANES), F32),
            pltpu.VMEM((padded, 16, LANES), F32),
            pltpu.VMEM((2, chips, 8, hidden_units), F32),
            part, part, part,
            pltpu.VMEM((row_count, 8, hidden_units), F32),
            pltpu.VMEM((2, 8, hidden_units), F32),
            pltpu.VMEM((2 * tile_count, LANES), F32),
            pltpu.VMEM((3 * tile_count, LANES), F32),
            pltpu.VMEM((blocks, LANES), F32),
            pltpu.VMEM((feats, rows_here), BF16),
            pltpu.VMEM((feats, rows_here), BF16),
            pltpu.SemaphoreType.DMA((CHUNKS,)),
            pltpu.SemaphoreType.DMA((10,)),
            pltpu.SemaphoreType.DMA((10,)),
        ],
        compiler_params=pltpu.CompilerParams(
            collective_id=0, has_side_effects=True, vmem_limit_bytes=48 << 20
        ),
    )(
        by_col, adjacency, tile_dst, tile_peer, tile_slot, offers, labels.reshape(4, LANES),
        w_self, w_neigh, w_class,
    )
    grad_features = (
        grad.reshape(col_count, feat_cols, 4, LANES)
        .transpose(1, 0, 2, 3)
        .reshape(feat_cols, node_rows)
    )
    return grad_features, grad_self, grad_neigh, grad_class


def solution(mesh):
    in_specs = (
        P("col", "row"),
        P("row", None, None, None),
        P("row", None),
        P("row", None),
        P("row", None),
        P("row", None, None),
        P(("row", "col")),
        P(),
        P(),
        P(),
    )
    out_specs = (P("col", "row"), P("col", None), P("col", None), P("col", None))
    return jax.shard_map(body, mesh=mesh, in_specs=in_specs, out_specs=out_specs, check_vma=False)
```

```python
import functools

import jax
import jax.numpy as jnp
from jax import lax
from jax.experimental import pallas as pl
from jax.experimental.pallas import tpu as pltpu
from jax.sharding import PartitionSpec as P

MESH = pl.DeviceIdType.MESH
F32 = jnp.float32
BF16 = jnp.bfloat16
LANES = 128
CHUNKS = 8

OFFERED, FEATURES, AGGREGATE, NEIGH_BACK, SELF_BACK, RETURNED, SWAP, CHIPS, ROWS = range(9)

INNER = (((1,), (0,)), ((), ()))
LAST = (((1,), (1,)), ((), ()))


def dot(a, b, dims=INNER):
    return lax.dot_general(a, b, dims, preferred_element_type=F32)


def split_dot(onehot, values):
    high = values.astype(BF16)
    low = (values - high.astype(F32)).astype(BF16)
    return dot(onehot, high) + dot(onehot, low)


def onehot(condition):
    return jnp.where(condition, 1.0, 0.0).astype(BF16)


def iota(shape, axis):
    return lax.broadcasted_iota(jnp.int32, shape, axis)


def layer_kernel(
    scale,
    feat_hbm, adjacency_ref, dst_hbm, peer_hbm, slot_hbm, offers_hbm, labels_hbm,
    w_self_hbm, w_neigh_hbm, w_class_hbm,
    grad_ref, grad_self_ref, grad_neigh_ref, grad_class_ref,
    feat_ref, dst_ref, peer_ref, slot_ref, offers_ref, labels_ref, w_self_ref, w_neigh_ref, w_class_ref,
    raw, tiles,
    offer_pad, pick_offer, put_offer, pick_source, put_source, pick_dest, put_dest, put_degree,
    to_nodes, to_columns, pick_rows,
    w_self_t, w_neigh_t, w_class_p, w_class_t,
    offered, incoming, feat_recv, agg_send, agg_recv, neigh_send, neigh_recv, self_send, self_recv,
    slot_send, slot_recv, weights, half, mine, got, sums,
    gathered, products, degree, x_self, x_neigh,
    tile_sem, input_sem, send, recv,
):
    row_count, col_count = lax.axis_size("row"), lax.axis_size("col")
    chip_count = col_count // 2
    row, col = lax.axis_index("row"), lax.axis_index("col")
    chip, core = col // 2, col % 2
    sibling = (row, chip * 2 + 1 - core)
    node_rows = col_count * 8
    tile_count = raw.shape[0]
    octs = tile_count // 8
    slot_rows = row_count * 16
    padded = incoming.shape[0] * 16

    def col_at(step):
        other = lax.rem(col + step, col_count)
        return other, (row, other)

    def row_at(step):
        other = lax.rem(row + step, row_count)
        return other, (other, col)

    def chip_at(step):
        other = lax.rem(chip + step, chip_count)
        return other, (row, other * 2 + core)

    def far_first(step, count):
        return count // 2 + (step // 2) * (2 * (step % 2) - 1)

    def remote(source, target, phase, device):
        return pltpu.make_async_remote_copy(
            source, target, send.at[phase], recv.at[phase], device_id=device, device_id_type=MESH
        )

    def scatter(source, target, phase, count, at, here):
        @pl.loop(1, count)
        def _(step):
            other, device = at(far_first(step, count))
            remote(source.at[other], target.at[here], phase, device).start()

        target[here] = source[here]

    def wait_for(target, count, semaphore):
        others = target.at[pl.ds(0, count - 1)]
        pltpu.make_async_copy(others, others, semaphore).wait()

    barrier = pltpu.get_barrier_semaphore()

    @pl.loop(1, row_count)
    def _(step):
        pl.semaphore_signal(barrier, inc=1, device_id=row_at(far_first(step, row_count))[1], device_id_type=MESH)

    @pl.loop(1, col_count)
    def _(step):
        pl.semaphore_signal(barrier, inc=1, device_id=col_at(far_first(step, col_count))[1], device_id_type=MESH)

    loads = [
        pltpu.make_async_copy(hbm, vmem, input_sem.at[number])
        for number, (hbm, vmem) in enumerate((
            (offers_hbm, offers_ref), (feat_hbm, feat_ref), (dst_hbm, dst_ref), (peer_hbm, peer_ref),
            (slot_hbm, slot_ref), (labels_hbm, labels_ref), (w_self_hbm, w_self_ref),
            (w_neigh_hbm, w_neigh_ref), (w_class_hbm, w_class_ref),
        ))
    ]
    for load in loads:
        load.start()

    per_chunk = tile_count // CHUNKS

    def chunk_copy(part):
        place = pl.ds(part * per_chunk, per_chunk)
        return pltpu.make_async_copy(adjacency_ref.at[0, place], raw.at[place], tile_sem.at[part])

    for part in range(CHUNKS):
        chunk_copy(part).start()

    offer_pad[...] = jnp.zeros_like(offer_pad)
    loads[0].wait()
    slots, peers = offers_ref.shape
    offer_pad[0:slots, 0:peers] = offers_ref[...].astype(F32)
    place = iota((padded, slots), 0)
    offer_rows = dot(
        onehot(place % slots == iota((padded, slots), 1)), offer_pad[...].astype(BF16)
    )
    place = iota((padded, LANES), 0)
    offer_col = jnp.sum(
        jnp.where(place // 16 == iota((padded, LANES), 1), offer_rows, 0.0), axis=1, keepdims=True
    ).astype(jnp.int32)
    place_col = iota((padded, 1), 0)
    offer_col = jnp.where(
        place_col < slot_rows, offer_col * 2 + (place_col // slots) % 2, -1
    )
    pick = jnp.where(offer_col == iota((padded, node_rows), 1), 1.0, 0.0)
    pick_offer[...] = pick.astype(BF16)
    loads[1].wait()
    offered[...] = (
        dot(pick_offer[...], feat_ref[...].reshape(node_rows, LANES))
        .astype(BF16)
        .reshape(offered.shape)
    )
    incoming[row_count:] = jnp.zeros_like(incoming[row_count:])
    slot_recv[row_count:] = jnp.zeros_like(slot_recv[row_count:])

    pl.semaphore_wait(barrier, row_count + col_count - 2)
    scatter(offered, incoming, OFFERED, row_count, row_at, row)
    scatter(feat_ref, feat_recv, FEATURES, col_count, col_at, col)

    put_offer[...] = pick.T.astype(BF16)
    for load in loads[2:]:
        load.wait()
    dst = dst_ref[...]
    source = peer_ref[...] * 16 + slot_ref[...]
    dst_rows = jnp.concatenate([dst * 2, dst * 2 + 1], axis=1)
    source_rows = jnp.concatenate([source, source + 8], axis=1)
    pairs = dst_rows.shape[1]
    square = iota((pairs, pairs), 0) == iota((pairs, pairs), 1)

    def column(values):
        return jnp.sum(jnp.where(square, values, 0), axis=1, keepdims=True)

    put_dest[...] = onehot(iota((node_rows, pairs), 0) == dst_rows)
    pick_dest[...] = onehot(iota((pairs, node_rows), 1) == column(dst_rows))
    put_source[...] = onehot(iota((padded, pairs), 0) == source_rows)
    pick_source[...] = onehot(iota((pairs, padded), 1) == column(source_rows))
    block_of = iota((node_rows, tile_count), 0)
    put_degree[...] = onehot(block_of // 2 == dst)
    feat_count = col_count * 2

    def received_row(place):
        feature = place % feat_count
        return (feature // 2) * 8 + (place // feat_count) * 2 + feature % 2

    one, two = iota((node_rows, 2 * feat_count), 0), iota((node_rows, 2 * feat_count), 1)
    owner = ((one % (4 * col_count)) // 8) * 2 + one // (4 * col_count)
    kind = one % 8
    pick_rows[0] = onehot(
        (kind < 4) & (two == owner * 2 + kind % 2 + (kind // 2) * feat_count)
    )
    pick_rows[1] = onehot((kind >= 4) & (two == owner * 4 + kind - 4))
    one, two = iota((node_rows, node_rows), 0), iota((node_rows, node_rows), 1)
    to_nodes[...] = onehot(two == received_row(one))
    to_columns[...] = onehot(one == received_row(two))
    w_self_t[...] = w_self_ref[...].astype(F32).T.astype(BF16)
    w_neigh_t[...] = w_neigh_ref[...].astype(F32).T.astype(BF16)
    class_count, hidden_units = w_class_ref.shape
    class_rows = w_class_t.shape[0]
    w_class_t[...] = jnp.zeros_like(w_class_t)
    w_class_t[0:class_count] = w_class_ref[...]
    w_class_p[...] = jnp.zeros_like(w_class_p)
    w_class_p[:, 0:class_rows] = w_class_t[...].astype(F32).T.astype(BF16)

    for part in range(CHUNKS):
        chunk_copy(part).wait()
        for oct_ in range(part * octs // CHUNKS, (part + 1) * octs // CHUNKS):
            for k in range(8):
                tiles[oct_, k // 2 * LANES : (k // 2 + 1) * LANES, k % 2 * LANES : (k % 2 + 1) * LANES] = (
                    raw[oct_ * 8 + k].astype(F32).astype(BF16)
                )

    def oct_products(lines, oct_):
        kinds = iota(lines.shape, 0) % 8
        left = jnp.concatenate(
            [jnp.where(kinds % 2 == half_, lines, 0.0) for half_ in range(2)], axis=1
        ).astype(BF16)
        out = dot(left, tiles[oct_], LAST)
        kept = out[:, 0:LANES]
        for quarter in range(1, 4):
            kept = jnp.where(
                kinds // 2 == quarter, out[:, quarter * LANES : (quarter + 1) * LANES], kept
            )
        return kept

    def tile_lines(oct_):
        return [
            gathered[kind * tile_count + 8 * oct_ : kind * tile_count + 8 * oct_ + 8]
            for kind in range(2)
        ]

    def keep(oct_, kept):
        for kind in range(2):
            at = kind * tile_count + 8 * oct_
            products[at : at + 8] = kept[8 * kind : 8 * kind + 8]

    ones = jnp.ones((8, LANES), F32)
    for oct_ in range(octs):
        products[8 * oct_ : 8 * oct_ + 8] = oct_products(ones, oct_)
    degree[...] = jnp.maximum(split_dot(put_degree[...], products[0:tile_count]), 1.0)

    wait_for(incoming, row_count, recv.at[OFFERED])
    gathered[...] = dot(pick_source[...], incoming[...].reshape(padded, LANES))
    for oct_ in range(octs):
        keep(oct_, oct_products(jnp.concatenate(tile_lines(oct_), axis=0), oct_))
    agg_send[...] = (
        (split_dot(put_dest[...], products[...]) / degree[...])
        .astype(BF16)
        .reshape(agg_send.shape)
    )
    scatter(agg_send, agg_recv, AGGREGATE, col_count, col_at, col)

    def node_columns(received, x_ref):
        moved = dot(to_nodes[...], received[...].reshape(node_rows, LANES)).astype(BF16)
        for block in range(4):
            x_ref[:, block * LANES : (block + 1) * LANES] = moved[
                block * feat_count : (block + 1) * feat_count
            ]

    wait_for(feat_recv, col_count, recv.at[FEATURES])
    node_columns(feat_recv, x_self)
    pre_self = dot(w_self_t[...], x_self[...])
    wait_for(agg_recv, col_count, recv.at[AGGREGATE])
    node_columns(agg_recv, x_neigh)

    pre = pre_self + dot(w_neigh_t[...], x_neigh[...])
    sigmoid = 1.0 / (1.0 + jnp.exp(-pre))
    hidden = (pre * sigmoid).astype(BF16)
    logits = dot(w_class_t[...], hidden)
    classes = iota(logits.shape, 0)
    exponent = jnp.where(classes < class_count, jnp.exp(logits), 0.0)
    soft = exponent / jnp.sum(exponent, axis=0, keepdims=True)
    label_row = jnp.concatenate([labels_ref[block : block + 1] for block in range(4)], axis=1)
    dlogits = (soft - jnp.where(classes == label_row, 1.0, 0.0)).astype(BF16)
    slope = sigmoid * (1.0 + pre * (1.0 - sigmoid))
    dpre = (dot(w_class_p[:, 0:class_rows], dlogits) * slope).astype(BF16)

    def block_rows(values):
        stacked = jnp.concatenate(
            [values[:, block * LANES : (block + 1) * LANES] for block in range(4)], axis=0
        )
        return dot(to_columns[...], stacked).astype(BF16).reshape(neigh_send.shape)

    my_degree = degree[pl.ds(pl.multiple_of(col * 8, 8), 8)]
    my_divisor = jnp.concatenate([my_degree[2 * block : 2 * block + 1] for block in range(4)], axis=1)
    both = jnp.concatenate([x_self[...], x_neigh[...]], axis=0)
    left = jnp.concatenate(
        [dot(pick_rows[0], both).astype(BF16), dot(pick_rows[1], hidden).astype(BF16)], axis=1
    )
    filler = jnp.zeros((hidden_units - class_rows, dlogits.shape[1]), BF16)
    right = jnp.concatenate([dpre, jnp.concatenate([dlogits, filler], axis=0)], axis=1)
    weights[...] = (dot(left, right, LAST) * scale).reshape(weights.shape)
    swap = remote(weights.at[1 - core], half, SWAP, sibling)
    swap.start()
    neigh_send[...] = block_rows((dot(w_neigh_ref[...], dpre) / my_divisor).astype(BF16))
    scatter(neigh_send, neigh_recv, NEIGH_BACK, col_count, col_at, col)
    swap.wait()
    mine[...] = (weights[core] + half[...]).astype(BF16)
    scatter(mine, got, CHIPS, chip_count, chip_at, chip)

    self_send[...] = block_rows(dot(w_self_ref[...], dpre).astype(BF16))
    scatter(self_send, self_recv, SELF_BACK, col_count, col_at, col)

    wait_for(neigh_recv, col_count, recv.at[NEIGH_BACK])
    gathered[...] = dot(pick_dest[...], neigh_recv[...].reshape(node_rows, LANES))
    kinds = iota((16, LANES), 0) % 8
    for oct_ in range(octs):
        lines = jnp.concatenate(tile_lines(oct_), axis=0)
        left = jnp.concatenate(
            [jnp.where(kinds // 2 == quarter, lines, 0.0) for quarter in range(4)], axis=1
        ).astype(BF16)
        out = dot(left, tiles[oct_])
        keep(oct_, jnp.where(kinds % 2 == 0, out[:, 0:LANES], out[:, LANES : 2 * LANES]))
    slot_send[...] = (
        split_dot(put_source[...], products[...]).astype(BF16).reshape(slot_send.shape)
    )
    scatter(slot_send, slot_recv, RETURNED, row_count, row_at, row)

    wait_for(got, chip_count, recv.at[CHIPS])
    sums[row] = jnp.sum(got[...].astype(F32), axis=0).astype(BF16)

    @pl.loop(1, row_count)
    def _(step):
        device = row_at(far_first(step, row_count))[1]
        remote(sums.at[row], sums.at[row], ROWS, device).start()

    wait_for(self_recv, col_count, recv.at[SELF_BACK])
    wait_for(slot_recv, row_count, recv.at[RETURNED])
    landed = dot(put_offer[...], slot_recv[...].reshape(padded, LANES))
    grad_ref[...] = (
        (self_recv[...].reshape(node_rows, LANES).astype(F32) + landed)
        .astype(BF16)
        .reshape(grad_ref.shape)
    )
    wait_for(sums, row_count, recv.at[ROWS])
    total = jnp.sum(sums[...].astype(F32), axis=0)
    grad_self_ref[...] = total[0:2]
    grad_neigh_ref[...] = total[2:4]
    grad_class_ref[...] = total[4:8, 0:class_count]

    wait_for(incoming, row_count, send.at[OFFERED])
    for phase in (FEATURES, AGGREGATE, NEIGH_BACK, SELF_BACK):
        wait_for(feat_recv, col_count, send.at[phase])
    wait_for(slot_recv, row_count, send.at[RETURNED])
    wait_for(got, chip_count, send.at[CHIPS])
    wait_for(sums, row_count, send.at[ROWS])


def finish_kernel(*refs):
    count = (len(refs) - 2) // 3
    inputs, outputs, staged = refs[:count], refs[count : 2 * count], refs[2 * count : 3 * count]
    arrived, left = refs[-2:]

    def copies(sources, targets, semaphore):
        return [
            pltpu.make_async_copy(sources[number], targets[number], semaphore.at[number])
            for number in range(count)
        ]

    reads, writes = copies(inputs, staged, arrived), copies(staged, outputs, left)
    for read in reads:
        read.start()
    for read, write in zip(reads, writes):
        read.wait()
        write.start()
    for write in writes:
        write.wait()


def body(
    features_t, adjacency, tile_dst, tile_peer, tile_slot, offers, labels, w_self, w_neigh, w_class
):
    row_count = lax.axis_size("row")
    col_count = lax.axis_size("col")
    feat_cols, node_rows = features_t.shape
    tile_count = adjacency.shape[1]
    hidden_units, class_count = w_class.shape
    feats = feat_cols * col_count
    class_rows = -(-class_count // 16) * 16
    padded = -(-row_count // 8) * 8
    blocks = col_count * 8
    chips = col_count // 2
    rows_here = labels.shape[0]
    scale = (rows_here * row_count * col_count) ** (-0.5)
    by_col = (
        features_t.reshape(feat_cols, col_count * 4, LANES)
        .transpose(1, 0, 2)
        .reshape(col_count, 8, LANES)
    )
    vmem = pl.BlockSpec(memory_space=pltpu.VMEM)
    message = pltpu.VMEM((col_count, 8, LANES), BF16)
    part = pltpu.VMEM((chips, 8, hidden_units), F32)
    grad, grad_self, grad_neigh, grad_class = pl.pallas_call(
        functools.partial(layer_kernel, scale),
        out_shape=(
            jax.ShapeDtypeStruct((col_count, 8, LANES), BF16),
            jax.ShapeDtypeStruct((feat_cols, hidden_units), F32),
            jax.ShapeDtypeStruct((feat_cols, hidden_units), F32),
            jax.ShapeDtypeStruct((hidden_units // col_count, class_count), F32),
        ),
        in_specs=[pl.BlockSpec(memory_space=pl.ANY)] * 10,
        out_specs=(vmem,) * 4,
        scratch_shapes=[
            message,
            pltpu.VMEM(tile_dst.shape, jnp.int32),
            pltpu.VMEM(tile_peer.shape, jnp.int32),
            pltpu.VMEM(tile_slot.shape, jnp.int32),
            pltpu.VMEM(offers.shape[:0:-1], jnp.int32),
            pltpu.VMEM((4, LANES), jnp.int32),
            pltpu.VMEM(w_self.shape, BF16),
            pltpu.VMEM(w_neigh.shape, BF16),
            pltpu.VMEM((class_count, hidden_units), BF16),
            pltpu.VMEM((tile_count, LANES, LANES), jnp.int32),
            pltpu.VMEM((tile_count // 8, 4 * LANES, 2 * LANES), BF16),
            pltpu.VMEM((8, LANES), F32),
            pltpu.VMEM((padded * 16, blocks), BF16),
            pltpu.VMEM((blocks, padded * 16), BF16),
            pltpu.VMEM((2 * tile_count, padded * 16), BF16),
            pltpu.VMEM((padded * 16, 2 * tile_count), BF16),
            pltpu.VMEM((2 * tile_count, blocks), BF16),
            pltpu.VMEM((blocks, 2 * tile_count), BF16),
            pltpu.VMEM((blocks, tile_count), BF16),
            pltpu.VMEM((blocks, blocks), BF16),
            pltpu.VMEM((blocks, blocks), BF16),
            pltpu.VMEM((2, blocks, 2 * feats), BF16),
            pltpu.VMEM((hidden_units, feats), BF16),
            pltpu.VMEM((hidden_units, feats), BF16),
            pltpu.VMEM((hidden_units, hidden_units), BF16),
            pltpu.VMEM((class_rows, hidden_units), BF16),
            pltpu.VMEM((padded, 16, LANES), BF16),
            pltpu.VMEM((padded, 16, LANES), BF16),
            message, message, message, message, message, message, message,
            pltpu.VMEM((padded, 16, LANES), BF16),
            pltpu.VMEM((padded, 16, LANES), BF16),
            pltpu.VMEM((2, chips, 8, hidden_units), F32),
            part,
            pltpu.VMEM((chips, 8, hidden_units), BF16),
            pltpu.VMEM((chips, 8, hidden_units), BF16),
            pltpu.VMEM((row_count, 8, hidden_units), BF16),
            pltpu.VMEM((2 * tile_count, LANES), F32),
            pltpu.VMEM((2 * tile_count, LANES), F32),
            pltpu.VMEM((blocks, LANES), F32),
            pltpu.VMEM((feats, rows_here), BF16),
            pltpu.VMEM((feats, rows_here), BF16),
            pltpu.SemaphoreType.DMA((CHUNKS,)),
            pltpu.SemaphoreType.DMA((9,)),
            pltpu.SemaphoreType.DMA((9,)),
            pltpu.SemaphoreType.DMA((9,)),
        ],
        compiler_params=pltpu.CompilerParams(
            collective_id=0, has_side_effects=True, vmem_limit_bytes=60 << 20
        ),
    )(
        by_col, adjacency, tile_dst, tile_peer, tile_slot, offers[0].T, labels.reshape(4, LANES),
        w_self, w_neigh, w_class.T,
    )
    anywhere = pl.BlockSpec(memory_space=pl.ANY)
    results = (grad, grad_self, grad_neigh, grad_class)
    grad, grad_self, grad_neigh, grad_class = pl.pallas_call(
        finish_kernel,
        out_shape=tuple(jax.ShapeDtypeStruct(result.shape, result.dtype) for result in results),
        in_specs=[anywhere] * 4,
        out_specs=(anywhere,) * 4,
        scratch_shapes=[pltpu.VMEM(result.shape, result.dtype) for result in results]
        + [pltpu.SemaphoreType.DMA((4,))] * 2,
        compiler_params=pltpu.CompilerParams(vmem_limit_bytes=60 << 20),
    )(*results)
    grad_features = (
        grad.reshape(col_count * 4, feat_cols, LANES)
        .transpose(1, 0, 2)
        .reshape(feat_cols, node_rows)
    )
    return grad_features, grad_self, grad_neigh, grad_class


def solution(mesh):
    in_specs = (
        P("col", "row"),
        P("row", None, None, None),
        P("row", None),
        P("row", None),
        P("row", None),
        P("row", None, None),
        P(("row", "col")),
        P(),
        P(),
        P(),
    )
    out_specs = (P("col", "row"), P("col", None), P("col", None), P("col", None))
    return jax.shard_map(body, mesh=mesh, in_specs=in_specs, out_specs=out_specs, check_vma=False)
```

```python
import functools

import jax
import jax.numpy as jnp
from jax import lax
from jax.experimental import pallas as pl
from jax.experimental.pallas import tpu as pltpu
from jax.sharding import PartitionSpec as P

MESH = pl.DeviceIdType.MESH
F32 = jnp.float32
BF16 = jnp.bfloat16
LANES = 128
CHUNKS = 8

OFFERED, FEATURES, AGGREGATE, NEIGH_BACK, SELF_BACK, RETURNED, SWAP, CHIPS, ROWS = range(9)

INNER = (((1,), (0,)), ((), ()))
LAST = (((1,), (1,)), ((), ()))


def dot(a, b, dims=INNER):
    return lax.dot_general(a, b, dims, preferred_element_type=F32)


def split_dot(onehot, values):
    high = values.astype(BF16)
    low = (values - high.astype(F32)).astype(BF16)
    return dot(onehot, high) + dot(onehot, low)


def onehot(condition):
    return jnp.where(condition, 1.0, 0.0).astype(BF16)


def iota(shape, axis):
    return lax.broadcasted_iota(jnp.int32, shape, axis)


def layer_kernel(
    scale,
    feat_hbm, adjacency_ref, dst_hbm, peer_hbm, slot_hbm, offers_hbm, labels_hbm,
    w_self_hbm, w_neigh_hbm, w_class_hbm,
    grad_ref, grad_self_ref, grad_neigh_ref, grad_class_ref,
    feat_ref, dst_ref, peer_ref, slot_ref, offers_ref, labels_ref, w_self_ref, w_neigh_ref, w_class_ref,
    raw, tiles,
    offer_pad, pick_offer, put_offer, pick_source, put_source, pick_dest, put_dest, put_degree,
    to_nodes, to_columns, pick_rows,
    w_self_t, w_neigh_t, w_class_p, w_class_t,
    offered, incoming, feat_recv, agg_send, agg_recv, neigh_send, neigh_recv, self_send, self_recv,
    slot_send, slot_recv, weights, half, mine, got, sums,
    gathered, products, degree, x_self, x_neigh, rows_self,
    tile_sem, input_sem, send, recv,
):
    row_count, col_count = lax.axis_size("row"), lax.axis_size("col")
    chip_count = col_count // 2
    row, col = lax.axis_index("row"), lax.axis_index("col")
    chip, core = col // 2, col % 2
    sibling = (row, chip * 2 + 1 - core)
    node_rows = col_count * 8
    tile_count = raw.shape[0]
    octs = tile_count // 8
    slot_rows = row_count * 16
    padded = incoming.shape[0] * 16

    def col_at(step):
        other = lax.rem(col + step, col_count)
        return other, (row, other)

    def row_at(step):
        other = lax.rem(row + step, row_count)
        return other, (other, col)

    def chip_at(step):
        other = lax.rem(chip + step, chip_count)
        return other, (row, other * 2 + core)

    def far_first(step, count):
        return count // 2 + (step // 2) * (2 * (step % 2) - 1)

    def remote(source, target, phase, device):
        return pltpu.make_async_remote_copy(
            source, target, send.at[phase], recv.at[phase], device_id=device, device_id_type=MESH
        )

    def scatter(source, target, phase, count, at, here):
        @pl.loop(1, count)
        def _(step):
            other, device = at(far_first(step, count))
            remote(source.at[other], target.at[here], phase, device).start()

        target[here] = source[here]

    def wait_for(target, count, semaphore):
        others = target.at[pl.ds(0, count - 1)]
        pltpu.make_async_copy(others, others, semaphore).wait()

    barrier = pltpu.get_barrier_semaphore()

    @pl.loop(1, row_count)
    def _(step):
        pl.semaphore_signal(barrier, inc=1, device_id=row_at(far_first(step, row_count))[1], device_id_type=MESH)

    @pl.loop(1, col_count)
    def _(step):
        pl.semaphore_signal(barrier, inc=1, device_id=col_at(far_first(step, col_count))[1], device_id_type=MESH)

    loads = [
        pltpu.make_async_copy(hbm, vmem, input_sem.at[number])
        for number, (hbm, vmem) in enumerate((
            (offers_hbm, offers_ref), (feat_hbm, feat_ref), (dst_hbm, dst_ref), (peer_hbm, peer_ref),
            (slot_hbm, slot_ref), (labels_hbm, labels_ref), (w_self_hbm, w_self_ref),
            (w_neigh_hbm, w_neigh_ref), (w_class_hbm, w_class_ref),
        ))
    ]
    for load in loads:
        load.start()

    per_chunk = tile_count // CHUNKS

    def chunk_copy(part):
        place = pl.ds(part * per_chunk, per_chunk)
        return pltpu.make_async_copy(adjacency_ref.at[0, place], raw.at[place], tile_sem.at[part])

    for part in range(CHUNKS):
        chunk_copy(part).start()

    offer_pad[...] = jnp.zeros_like(offer_pad)
    loads[0].wait()
    slots, peers = offers_ref.shape
    offer_pad[0:slots, 0:peers] = offers_ref[...].astype(F32)
    place = iota((padded, slots), 0)
    offer_rows = dot(
        onehot(place % slots == iota((padded, slots), 1)), offer_pad[...].astype(BF16)
    )
    place = iota((padded, LANES), 0)
    offer_col = jnp.sum(
        jnp.where(place // 16 == iota((padded, LANES), 1), offer_rows, 0.0), axis=1, keepdims=True
    ).astype(jnp.int32)
    place_col = iota((padded, 1), 0)
    offer_col = jnp.where(
        place_col < slot_rows, offer_col * 2 + (place_col // slots) % 2, -1
    )
    pick = jnp.where(offer_col == iota((padded, node_rows), 1), 1.0, 0.0)
    pick_offer[...] = pick.astype(BF16)
    loads[1].wait()
    offered[...] = (
        dot(pick_offer[...], feat_ref[...].reshape(node_rows, LANES))
        .astype(BF16)
        .reshape(offered.shape)
    )
    incoming[row_count:] = jnp.zeros_like(incoming[row_count:])
    slot_recv[row_count:] = jnp.zeros_like(slot_recv[row_count:])

    pl.semaphore_wait(barrier, row_count + col_count - 2)
    scatter(offered, incoming, OFFERED, row_count, row_at, row)
    scatter(feat_ref, feat_recv, FEATURES, col_count, col_at, col)

    put_offer[...] = pick.T.astype(BF16)
    for load in loads[2:]:
        load.wait()
    dst = dst_ref[...]
    source = peer_ref[...] * 16 + slot_ref[...]
    dst_rows = jnp.concatenate([dst * 2, dst * 2 + 1], axis=1)
    source_rows = jnp.concatenate([source, source + 8], axis=1)
    pairs = dst_rows.shape[1]
    square = iota((pairs, pairs), 0) == iota((pairs, pairs), 1)

    def column(values):
        return jnp.sum(jnp.where(square, values, 0), axis=1, keepdims=True)

    put_dest[...] = onehot(iota((node_rows, pairs), 0) == dst_rows)
    pick_dest[...] = onehot(iota((pairs, node_rows), 1) == column(dst_rows))
    put_source[...] = onehot(iota((padded, pairs), 0) == source_rows)
    pick_source[...] = onehot(iota((pairs, padded), 1) == column(source_rows))
    block_of = iota((node_rows, tile_count), 0)
    put_degree[...] = onehot(block_of // 2 == dst)
    feat_count = col_count * 2

    def received_row(place):
        feature = place % feat_count
        return (feature // 2) * 8 + (place // feat_count) * 2 + feature % 2

    one, two = iota((node_rows, 2 * feat_count), 0), iota((node_rows, 2 * feat_count), 1)
    owner = ((one % (4 * col_count)) // 8) * 2 + one // (4 * col_count)
    kind = one % 8
    pick_rows[0] = onehot(
        (kind < 4) & (two == owner * 2 + kind % 2 + (kind // 2) * feat_count)
    )
    pick_rows[1] = onehot((kind >= 4) & (two == owner * 4 + kind - 4))
    one, two = iota((node_rows, node_rows), 0), iota((node_rows, node_rows), 1)
    to_nodes[...] = onehot(two == received_row(one))
    to_columns[...] = onehot(one == received_row(two))
    w_self_t[...] = w_self_ref[...].astype(F32).T.astype(BF16)
    w_neigh_t[...] = w_neigh_ref[...].astype(F32).T.astype(BF16)
    class_count, hidden_units = w_class_ref.shape
    class_rows = w_class_t.shape[0]
    w_class_t[...] = jnp.zeros_like(w_class_t)
    w_class_t[0:class_count] = w_class_ref[...]
    w_class_p[...] = jnp.zeros_like(w_class_p)
    w_class_p[:, 0:class_rows] = w_class_t[...].astype(F32).T.astype(BF16)

    for part in range(CHUNKS):
        chunk_copy(part).wait()
        for oct_ in range(part * octs // CHUNKS, (part + 1) * octs // CHUNKS):
            for k in range(8):
                tiles[oct_, k // 2 * LANES : (k // 2 + 1) * LANES, k % 2 * LANES : (k % 2 + 1) * LANES] = (
                    raw[oct_ * 8 + k].astype(F32).astype(BF16)
                )

    def oct_products(lines, oct_):
        kinds = iota(lines.shape, 0) % 8
        left = jnp.concatenate(
            [jnp.where(kinds % 2 == half_, lines, 0.0) for half_ in range(2)], axis=1
        ).astype(BF16)
        out = dot(left, tiles[oct_], LAST)
        kept = out[:, 0:LANES]
        for quarter in range(1, 4):
            kept = jnp.where(
                kinds // 2 == quarter, out[:, quarter * LANES : (quarter + 1) * LANES], kept
            )
        return kept

    def tile_lines(oct_):
        return [
            gathered[kind * tile_count + 8 * oct_ : kind * tile_count + 8 * oct_ + 8]
            for kind in range(2)
        ]

    def keep(oct_, kept):
        for kind in range(2):
            at = kind * tile_count + 8 * oct_
            products[at : at + 8] = kept[8 * kind : 8 * kind + 8]

    ones = jnp.ones((8, LANES), F32)
    for oct_ in range(octs):
        products[8 * oct_ : 8 * oct_ + 8] = oct_products(ones, oct_)
    degree[...] = jnp.maximum(split_dot(put_degree[...], products[0:tile_count]), 1.0)

    wait_for(incoming, row_count, recv.at[OFFERED])
    gathered[...] = dot(pick_source[...], incoming[...].reshape(padded, LANES))
    for oct_ in range(octs):
        keep(oct_, oct_products(jnp.concatenate(tile_lines(oct_), axis=0), oct_))
    agg_send[...] = (
        (split_dot(put_dest[...], products[...]) / degree[...])
        .astype(BF16)
        .reshape(agg_send.shape)
    )
    scatter(agg_send, agg_recv, AGGREGATE, col_count, col_at, col)

    def node_columns(received, x_ref):
        moved = dot(to_nodes[...], received[...].reshape(node_rows, LANES)).astype(BF16)
        for block in range(4):
            x_ref[:, block * LANES : (block + 1) * LANES] = moved[
                block * feat_count : (block + 1) * feat_count
            ]

    wait_for(feat_recv, col_count, recv.at[FEATURES])
    node_columns(feat_recv, x_self)
    pre_self = dot(w_self_t[...], x_self[...])
    rows_self[...] = dot(pick_rows[0, :, 0:feat_count], x_self[...]).astype(BF16)
    wait_for(agg_recv, col_count, recv.at[AGGREGATE])
    node_columns(agg_recv, x_neigh)

    pre = pre_self + dot(w_neigh_t[...], x_neigh[...])
    sigmoid = 1.0 / (1.0 + jnp.exp(-pre))
    hidden = (pre * sigmoid).astype(BF16)
    logits = dot(w_class_t[...], hidden)
    classes = iota(logits.shape, 0)
    exponent = jnp.where(classes < class_count, jnp.exp(logits), 0.0)
    soft = exponent / jnp.sum(exponent, axis=0, keepdims=True)
    label_row = jnp.concatenate([labels_ref[block : block + 1] for block in range(4)], axis=1)
    dlogits = (soft - jnp.where(classes == label_row, 1.0, 0.0)).astype(BF16)
    slope = sigmoid * (1.0 + pre * (1.0 - sigmoid))
    dpre = (dot(w_class_p[:, 0:class_rows], dlogits) * slope).astype(BF16)

    def block_rows(values):
        stacked = jnp.concatenate(
            [values[:, block * LANES : (block + 1) * LANES] for block in range(4)], axis=0
        )
        return dot(to_columns[...], stacked).astype(BF16).reshape(neigh_send.shape)

    my_degree = degree[pl.ds(pl.multiple_of(col * 8, 8), 8)]
    my_divisor = jnp.concatenate([my_degree[2 * block : 2 * block + 1] for block in range(4)], axis=1)
    neigh_send[...] = block_rows((dot(w_neigh_ref[...], dpre) / my_divisor).astype(BF16))
    scatter(neigh_send, neigh_recv, NEIGH_BACK, col_count, col_at, col)
    rows_neigh = dot(pick_rows[0, :, feat_count : 2 * feat_count], x_neigh[...]).astype(BF16)
    rows_class = dot(pick_rows[1], hidden).astype(BF16)
    filler = jnp.zeros((hidden_units - class_rows, dlogits.shape[1]), BF16)
    total = dot(rows_self[...] + rows_neigh, dpre, LAST) + dot(
        rows_class, jnp.concatenate([dlogits, filler], axis=0), LAST
    )
    weights[...] = (total * scale).reshape(weights.shape)
    swap = remote(weights.at[1 - core], half, SWAP, sibling)
    swap.start()
    self_send[...] = block_rows(dot(w_self_ref[...], dpre).astype(BF16))
    swap.wait()
    mine[...] = (weights[core] + half[...]).astype(BF16)
    scatter(mine, got, CHIPS, chip_count, chip_at, chip)

    scatter(self_send, self_recv, SELF_BACK, col_count, col_at, col)

    wait_for(neigh_recv, col_count, recv.at[NEIGH_BACK])
    gathered[...] = dot(pick_dest[...], neigh_recv[...].reshape(node_rows, LANES))
    kinds = iota((16, LANES), 0) % 8
    for oct_ in range(octs):
        lines = jnp.concatenate(tile_lines(oct_), axis=0)
        left = jnp.concatenate(
            [jnp.where(kinds // 2 == quarter, lines, 0.0) for quarter in range(4)], axis=1
        ).astype(BF16)
        out = dot(left, tiles[oct_])
        keep(oct_, jnp.where(kinds % 2 == 0, out[:, 0:LANES], out[:, LANES : 2 * LANES]))
    slot_send[...] = (
        split_dot(put_source[...], products[...]).astype(BF16).reshape(slot_send.shape)
    )
    scatter(slot_send, slot_recv, RETURNED, row_count, row_at, row)

    wait_for(got, chip_count, recv.at[CHIPS])
    sums[row] = jnp.sum(got[...].astype(F32), axis=0).astype(BF16)

    @pl.loop(1, row_count)
    def _(step):
        device = row_at(far_first(step, row_count))[1]
        remote(sums.at[row], sums.at[row], ROWS, device).start()

    wait_for(self_recv, col_count, recv.at[SELF_BACK])
    wait_for(slot_recv, row_count, recv.at[RETURNED])
    landed = dot(put_offer[...], slot_recv[...].reshape(padded, LANES))
    grad_ref[...] = (
        (self_recv[...].reshape(node_rows, LANES).astype(F32) + landed)
        .astype(BF16)
        .reshape(grad_ref.shape)
    )
    wait_for(sums, row_count, recv.at[ROWS])
    total = jnp.sum(sums[...].astype(F32), axis=0)
    grad_self_ref[...] = total[0:2]
    grad_neigh_ref[...] = total[2:4]
    grad_class_ref[...] = total[4:8, 0:class_count]

    wait_for(incoming, row_count, send.at[OFFERED])
    for phase in (FEATURES, AGGREGATE, NEIGH_BACK, SELF_BACK):
        wait_for(feat_recv, col_count, send.at[phase])
    wait_for(slot_recv, row_count, send.at[RETURNED])
    wait_for(got, chip_count, send.at[CHIPS])
    wait_for(sums, row_count, send.at[ROWS])


def finish_kernel(*refs):
    count = (len(refs) - 2) // 3
    inputs, outputs, staged = refs[:count], refs[count : 2 * count], refs[2 * count : 3 * count]
    arrived, left = refs[-2:]

    def copies(sources, targets, semaphore):
        return [
            pltpu.make_async_copy(sources[number], targets[number], semaphore.at[number])
            for number in range(count)
        ]

    reads, writes = copies(inputs, staged, arrived), copies(staged, outputs, left)
    for read in reads:
        read.start()
    for read, write in zip(reads, writes):
        read.wait()
        write.start()
    for write in writes:
        write.wait()


def body(
    features_t, adjacency, tile_dst, tile_peer, tile_slot, offers, labels, w_self, w_neigh, w_class
):
    row_count = lax.axis_size("row")
    col_count = lax.axis_size("col")
    feat_cols, node_rows = features_t.shape
    tile_count = adjacency.shape[1]
    hidden_units, class_count = w_class.shape
    feats = feat_cols * col_count
    class_rows = -(-class_count // 16) * 16
    padded = -(-row_count // 8) * 8
    blocks = col_count * 8
    chips = col_count // 2
    rows_here = labels.shape[0]
    scale = (rows_here * row_count * col_count) ** (-0.5)
    by_col = (
        features_t.reshape(feat_cols, col_count * 4, LANES)
        .transpose(1, 0, 2)
        .reshape(col_count, 8, LANES)
    )
    vmem = pl.BlockSpec(memory_space=pltpu.VMEM)
    message = pltpu.VMEM((col_count, 8, LANES), BF16)
    part = pltpu.VMEM((chips, 8, hidden_units), F32)
    grad, grad_self, grad_neigh, grad_class = pl.pallas_call(
        functools.partial(layer_kernel, scale),
        out_shape=(
            jax.ShapeDtypeStruct((col_count, 8, LANES), BF16),
            jax.ShapeDtypeStruct((feat_cols, hidden_units), F32),
            jax.ShapeDtypeStruct((feat_cols, hidden_units), F32),
            jax.ShapeDtypeStruct((hidden_units // col_count, class_count), F32),
        ),
        in_specs=[pl.BlockSpec(memory_space=pl.ANY)] * 10,
        out_specs=(vmem,) * 4,
        scratch_shapes=[
            message,
            pltpu.VMEM(tile_dst.shape, jnp.int32),
            pltpu.VMEM(tile_peer.shape, jnp.int32),
            pltpu.VMEM(tile_slot.shape, jnp.int32),
            pltpu.VMEM(offers.shape[:0:-1], jnp.int32),
            pltpu.VMEM((4, LANES), jnp.int32),
            pltpu.VMEM(w_self.shape, BF16),
            pltpu.VMEM(w_neigh.shape, BF16),
            pltpu.VMEM((class_count, hidden_units), BF16),
            pltpu.VMEM((tile_count, LANES, LANES), jnp.int32),
            pltpu.VMEM((tile_count // 8, 4 * LANES, 2 * LANES), BF16),
            pltpu.VMEM((8, LANES), F32),
            pltpu.VMEM((padded * 16, blocks), BF16),
            pltpu.VMEM((blocks, padded * 16), BF16),
            pltpu.VMEM((2 * tile_count, padded * 16), BF16),
            pltpu.VMEM((padded * 16, 2 * tile_count), BF16),
            pltpu.VMEM((2 * tile_count, blocks), BF16),
            pltpu.VMEM((blocks, 2 * tile_count), BF16),
            pltpu.VMEM((blocks, tile_count), BF16),
            pltpu.VMEM((blocks, blocks), BF16),
            pltpu.VMEM((blocks, blocks), BF16),
            pltpu.VMEM((2, blocks, 2 * feats), BF16),
            pltpu.VMEM((hidden_units, feats), BF16),
            pltpu.VMEM((hidden_units, feats), BF16),
            pltpu.VMEM((hidden_units, hidden_units), BF16),
            pltpu.VMEM((class_rows, hidden_units), BF16),
            pltpu.VMEM((padded, 16, LANES), BF16),
            pltpu.VMEM((padded, 16, LANES), BF16),
            message, message, message, message, message, message, message,
            pltpu.VMEM((padded, 16, LANES), BF16),
            pltpu.VMEM((padded, 16, LANES), BF16),
            pltpu.VMEM((2, chips, 8, hidden_units), F32),
            part,
            pltpu.VMEM((chips, 8, hidden_units), BF16),
            pltpu.VMEM((chips, 8, hidden_units), BF16),
            pltpu.VMEM((row_count, 8, hidden_units), BF16),
            pltpu.VMEM((2 * tile_count, LANES), F32),
            pltpu.VMEM((2 * tile_count, LANES), F32),
            pltpu.VMEM((blocks, LANES), F32),
            pltpu.VMEM((feats, rows_here), BF16),
            pltpu.VMEM((feats, rows_here), BF16),
            pltpu.VMEM((blocks, rows_here), BF16),
            pltpu.SemaphoreType.DMA((CHUNKS,)),
            pltpu.SemaphoreType.DMA((9,)),
            pltpu.SemaphoreType.DMA((9,)),
            pltpu.SemaphoreType.DMA((9,)),
        ],
        compiler_params=pltpu.CompilerParams(
            collective_id=0, has_side_effects=True, vmem_limit_bytes=60 << 20
        ),
    )(
        by_col, adjacency, tile_dst, tile_peer, tile_slot, offers[0].T, labels.reshape(4, LANES),
        w_self, w_neigh, w_class.T,
    )
    anywhere = pl.BlockSpec(memory_space=pl.ANY)
    results = (grad, grad_self, grad_neigh, grad_class)
    grad, grad_self, grad_neigh, grad_class = pl.pallas_call(
        finish_kernel,
        out_shape=tuple(jax.ShapeDtypeStruct(result.shape, result.dtype) for result in results),
        in_specs=[anywhere] * 4,
        out_specs=(anywhere,) * 4,
        scratch_shapes=[pltpu.VMEM(result.shape, result.dtype) for result in results]
        + [pltpu.SemaphoreType.DMA((4,))] * 2,
        compiler_params=pltpu.CompilerParams(vmem_limit_bytes=60 << 20),
    )(*results)
    grad_features = (
        grad.reshape(col_count * 4, feat_cols, LANES)
        .transpose(1, 0, 2)
        .reshape(feat_cols, node_rows)
    )
    return grad_features, grad_self, grad_neigh, grad_class


def solution(mesh):
    in_specs = (
        P("col", "row"),
        P("row", None, None, None),
        P("row", None),
        P("row", None),
        P("row", None),
        P("row", None, None),
        P(("row", "col")),
        P(),
        P(),
        P(),
    )
    out_specs = (P("col", "row"), P("col", None), P("col", None), P("col", None))
    return jax.shard_map(body, mesh=mesh, in_specs=in_specs, out_specs=out_specs, check_vma=False)
```
